32 devices in a mesh: row: 8 (over y, x, core), col: 4 (over z).
Axes of the slice: x: 2, y: 2, z: 4, core: 2. Of those that a mesh axis runs over, the one named last changes fastest.
Arguments:
- slab_u: bfloat16 [16, 4, 1408, 256], P('row', 'col'), may hold values from -6 to 6
- slab_v: bfloat16 [16, 4, 1408, 256], P('row', 'col'), may hold values from -0.15625 to 0.15625
- slab_rank: int32 [16, 4], P('row', 'col'), may hold values from 42 to 256, as said below
- panel_u: bfloat16 [2, 16, 1408, 256], P(None, 'row', 'col'), may hold values from -6 to 6
- panel_v: bfloat16 [2, 16, 1408, 256], P(None, 'row', 'col'), may hold values from -0.15625 to 0.15625
- panel_rank: int32 [2, 16], P(None, 'row'), may hold values from 42 to 256, as said below
- inverse_block: bfloat16 [2, 1408, 1408], P(None, 'col'), as said below
- column_tiles: int32 [4], P('col'), may hold values from 0 to 15, as said below
- sketch: bfloat16 [1408, 256], replicated, may hold values from -0.15625 to 0.15625
Outputs:
- basis_out: bfloat16 [16, 4, 1408, 256], P('row', 'col')
- coeff_out: bfloat16 [16, 4, 1408, 256], P('row', 'col')
The draws below stay inside these ranges and needn't reach their ends.
Inputs may be any that keep to these rules, and one draw needn't show every extreme that they name: `slab_rank`: columns of a slab tile's left factor at or past its rank are ignored. `panel_rank`: columns of a panel tile's left factor at or past its rank are ignored. `column_tiles`: entries are distinct tile rows of the slab. `inverse_block`: each block is lower triangular with a positive diagonal.
All inputs are finite; a program needn't handle non-finite values.
Results may differ from the reference program's by a relative error of at most 0.015.
Values may be sent and summed in bfloat16 or wider, within the bound.
A program may use at most 128 MiB of HBM per device.

```python
import jax
import jax.numpy as jnp
from jax import lax

TILE_WIDTH = 1408
RANK_MAX = 256
PANELS = 2
TILE_ROWS = 16
TILE_COLS = 4


def draw_rank_table(key, shape):
    values = jax.random.randint(key, shape, RANK_MAX // 6, RANK_MAX + 1, dtype=jnp.int32)
    values = values.at[0, 0].set(RANK_MAX)
    values = values.at[shape[0] - 1, shape[1] - 1].set(RANK_MAX // 6)
    return values


def draw_slab_rank(key, part):
    key = jax.random.fold_in(key, 3)
    return draw_rank_table(key, (TILE_ROWS, TILE_COLS))


def draw_panel_rank(key, part):
    key = jax.random.fold_in(key, 5)
    return draw_rank_table(key, (PANELS, TILE_ROWS))


def draw_column_tiles(key, part):
    key = jax.random.fold_in(key, 7)
    others = 1 + jax.random.permutation(key, jnp.arange(TILE_ROWS - 2, dtype=jnp.int32))
    first = jnp.full((1,), TILE_ROWS - 1, dtype=jnp.int32)
    second = jnp.zeros((1,), dtype=jnp.int32)
    return jnp.concatenate([first, second, others[:TILE_COLS - 2]]).astype(jnp.int32)


def draw_inverse_block(key, part):
    key = jax.random.fold_in(key, 11)
    key_off, key_diag = jax.random.split(key)
    index = jnp.arange(TILE_WIDTH, dtype=jnp.int32)
    below = index[:, None] > index[None, :]
    same = index[:, None] == index[None, :]
    off = 0.009 * jax.random.normal(key_off, (PANELS, TILE_WIDTH, TILE_WIDTH), jnp.float32)
    diag = jax.random.uniform(key_diag, (PANELS, TILE_WIDTH), jnp.float32, 0.08, 0.2)
    whole = jnp.where(below[None], off, 0.0) + jnp.where(same[None], diag[:, None, :], 0.0)
    return whole.astype(jnp.bfloat16)


def levels(key, extent, shards, low, top_value):
    loudness = 1.0
    for axis_at, shards_of in shards:
        heights = jax.random.uniform(jax.random.fold_in(jax.random.fold_in(key, 6), axis_at), (shards_of,), jnp.float32, low / len(shards), top_value / len(shards))
        loudness = loudness * jnp.repeat(jnp.exp(heights), extent[axis_at] // shards_of).reshape((-1,) + (1,) * (len(extent) - 1 - axis_at))
    return loudness


def bell_draw(stream_key, extent, width, bound, pieces=(), held_as=jnp.bfloat16):
    entries = width * jax.random.normal(stream_key, extent, jnp.float32)
    if pieces:
        entries = entries * levels(stream_key, extent, pieces, -0.22, 0.18)
    return jnp.clip(entries, -bound, bound).astype(held_as)


def setup_inputs(seed: int = 0) -> dict:
    streams_of = jax.random.split(jax.random.key(seed), 10)
    slab_u = bell_draw(streams_of[0], (TILE_ROWS, TILE_COLS, TILE_WIDTH, RANK_MAX), 1.0, 6.0, ((0, 8), (1, 4)))
    slab_v = bell_draw(streams_of[1], (TILE_ROWS, TILE_COLS, TILE_WIDTH, RANK_MAX), TILE_WIDTH ** -0.5, 0.15625, ((0, 8), (1, 4)))
    slab_rank = draw_slab_rank(jax.random.fold_in(streams_of[9], 71), 0)
    panel_u = bell_draw(streams_of[3], (PANELS, TILE_ROWS, TILE_WIDTH, RANK_MAX), 1.0, 6.0, ((1, 8), (2, 4)))
    panel_v = bell_draw(streams_of[4], (PANELS, TILE_ROWS, TILE_WIDTH, RANK_MAX), TILE_WIDTH ** -0.5, 0.15625, ((1, 8), (2, 4)))
    panel_rank = draw_panel_rank(jax.random.fold_in(streams_of[9], 71), 0)
    inverse_block = draw_inverse_block(jax.random.fold_in(streams_of[9], 71), 0)
    column_tiles = draw_column_tiles(jax.random.fold_in(streams_of[9], 71), 0)
    sketch = bell_draw(streams_of[8], (TILE_WIDTH, RANK_MAX), TILE_WIDTH ** -0.5, 0.15625)
    return dict(slab_u=slab_u, slab_v=slab_v, slab_rank=slab_rank, panel_u=panel_u, panel_v=panel_v, panel_rank=panel_rank, inverse_block=inverse_block, column_tiles=column_tiles, sketch=sketch)


def mask_columns(factor, rank):
    columns = jnp.arange(factor.shape[-1], dtype=jnp.int32)
    keep = (columns < rank).astype(factor.dtype)
    return factor * keep

def update_tile(tile_u, tile_v, tile_rank, row_u, row_v, side_u, side_v, sketch):
    masked_slab = mask_columns(tile_u, tile_rank)
    lefts = [masked_slab]
    rights = [tile_v]
    for panel in range(row_u.shape[0]):
        cross = jnp.dot(row_v[panel].T.astype(jnp.float32), side_v[panel].astype(jnp.float32), preferred_element_type=jnp.float32).astype(jnp.bfloat16)
        update = jnp.dot(side_u[panel].astype(jnp.float32), cross.T.astype(jnp.float32), preferred_element_type=jnp.float32).astype(jnp.bfloat16)
        lefts.append(row_u[panel])
        rights.append(-update)
    left_cat = jnp.concatenate(lefts, axis=1)
    right_cat = jnp.concatenate(rights, axis=1)
    small = jnp.dot(right_cat.T.astype(jnp.float32), sketch.astype(jnp.float32), preferred_element_type=jnp.float32).astype(jnp.bfloat16)
    image = jnp.dot(left_cat.astype(jnp.float32), small.astype(jnp.float32), preferred_element_type=jnp.float32)
    gram = jnp.dot(image.T.astype(jnp.float32), image.astype(jnp.float32), precision=lax.Precision.HIGHEST, preferred_element_type=jnp.float32)
    gram = gram + jnp.eye(gram.shape[0], dtype=jnp.float32)
    factor = jnp.linalg.cholesky(gram)
    basis = lax.linalg.triangular_solve(factor, image, left_side=False, lower=True, transpose_a=True)
    scale_basis = jnp.sqrt(jnp.float32(tile_u.shape[0]))
    basis_out = (basis * scale_basis).astype(jnp.bfloat16)
    basis_low = basis.astype(jnp.bfloat16)
    project = jnp.dot(left_cat.T.astype(jnp.float32), basis_low.astype(jnp.float32), preferred_element_type=jnp.float32).astype(jnp.bfloat16)
    coeff_out = jnp.dot(right_cat.astype(jnp.float32), project.astype(jnp.float32), preferred_element_type=jnp.float32).astype(jnp.bfloat16)
    return (basis_out, coeff_out)

def reference(slab_u, slab_v, slab_rank, panel_u, panel_v, panel_rank, inverse_block, column_tiles, sketch):
    masked_panel = mask_columns(panel_u, panel_rank[:, :, None, None])
    solved = jnp.einsum('pab,ptbr->ptar', inverse_block.astype(jnp.float32), panel_v.astype(jnp.float32)).astype(jnp.bfloat16)

    def tile_row(row_index):
        row_u = masked_panel[:, row_index]
        row_v = solved[:, row_index]

        def tile_col(col_index):
            source = column_tiles[col_index]
            return update_tile(slab_u[row_index, col_index], slab_v[row_index, col_index], slab_rank[row_index, col_index], row_u, row_v, masked_panel[:, source], solved[:, source], sketch)
        return lax.map(tile_col, jnp.arange(TILE_COLS, dtype=jnp.int32))
    basis_out, coeff_out = lax.map(tile_row, jnp.arange(TILE_ROWS, dtype=jnp.int32))
    return (basis_out, coeff_out)
```

```python
import jax
import jax.numpy as jnp
from jax import lax
from jax.experimental import pallas as pl
from jax.experimental.pallas import tpu as pltpu
from jax.sharding import PartitionSpec as P

F32 = jnp.float32
BF16 = jnp.bfloat16
GROUP = 4
BLOCK = 128


def mask_columns(factor, rank):
    columns = jnp.arange(factor.shape[-1], dtype=jnp.int32)
    keep = (columns < rank).astype(factor.dtype)
    return factor * keep


def invert_blocks(blocks):
    n = blocks[0].shape[0]
    lane_row = lax.broadcasted_iota(jnp.int32, (1, n), 1)
    many = range(len(blocks))
    left = list(blocks)
    done = [[] for _ in many]
    top = 0
    for j in range(0, n, GROUP):
        start = (j // 8) * 8
        if start > top:
            left = [t[start - top :] for t in left]
            top = start
        rows = n - top
        at = j - top
        row_index = lax.broadcasted_iota(jnp.int32, (rows, n), 0) + top
        lane = lax.broadcasted_iota(jnp.int32, (rows, n), 1)
        inside = (lane >= j) & (lane < j + GROUP)
        for b in many:
            t = left[b]
            col = [
                jnp.broadcast_to(t[:, j + s : j + s + 1], (rows, n)) for s in range(GROUP)
            ]
            row = [t[at + s : at + s + 1, :] for s in range(GROUP)]
            new = jnp.where(inside, 0.0, t)
            for s in range(GROUP):
                pivot = col[s][at + s : at + s + 1, :]
                comb = jnp.where(lane_row == j + s, 1.0, row[s])
                times = jnp.where(row_index > j + s, col[s] / pivot, 0.0)
                for u in range(s + 1, GROUP):
                    col[u] = col[u] - times * col[u][at + s : at + s + 1, :]
                    here = jnp.where(lane_row == j + s, 0.0, row[u])
                    row[u] = here - times[at + u : at + u + 1, :] * comb
                later = (lane_row > j + s) & (lane_row < j + GROUP)
                new = new - times * jnp.where(later, 0.0, comb)
                done[b].append(
                    jnp.where(lane_row <= j + s, comb, 0.0) * lax.rsqrt(pivot)
                )
            left[b] = new
    return [jnp.concatenate(rows_of, axis=0) for rows_of in done]


def full_dot(a, b, dims):
    return lax.dot_general(
        a, b, (dims, ((), ())), precision=lax.Precision.HIGHEST, preferred_element_type=F32
    )


def factor_kernel(gram_ref, out_ref):
    tiles = gram_ref.shape[0]
    n = gram_ref.shape[1]
    half = n // 2
    many = range(tiles)
    first = invert_blocks([gram_ref[b, :half, :half] for b in many])
    lower = [full_dot(gram_ref[b, half:, :half], first[b], ((1,), (1,))) for b in many]
    rest = [
        gram_ref[b, half:, half:] - full_dot(lower[b], lower[b], ((1,), (1,))) for b in many
    ]
    second = invert_blocks(rest)
    for b in many:
        corner = full_dot(lower[b], first[b], ((1,), (0,)))
        out_ref[b, :half, :half] = first[b]
        out_ref[b, :half, half:] = jnp.zeros((half, half), F32)
        out_ref[b, half:, :half] = -full_dot(second[b], corner, ((1,), (0,)))
        out_ref[b, half:, half:] = second[b]


def invert_factor(gram):
    tiles, n, _ = gram.shape
    step = 2 if tiles % 2 == 0 else 1
    return pl.pallas_call(
        factor_kernel,
        grid=(tiles // step,),
        out_shape=jax.ShapeDtypeStruct(gram.shape, F32),
        in_specs=[pl.BlockSpec((step, n, n), lambda i: (i, 0, 0))],
        out_specs=pl.BlockSpec((step, n, n), lambda i: (i, 0, 0)),
        compiler_params=pltpu.CompilerParams(vmem_limit_bytes=32 * 1024 * 1024),
        cost_estimate=pl.CostEstimate(
            flops=tiles * n * n * n, bytes_accessed=2 * gram.size * 4, transcendentals=0
        ),
    )(gram)


def dot(spec, a, b):
    return jnp.einsum(spec, a, b, preferred_element_type=F32)


def shards(
    slab_u, slab_v, slab_rank, panel_u, panel_v, panel_rank, inverse_block, column_tiles, sketch
):
    rows_here = panel_u.shape[1]
    panels = panel_u.shape[0]
    width = sketch.shape[0]
    me = lax.axis_index("row")
    targets = lax.all_gather(column_tiles, "col", axis=0, tiled=True)
    raw_v = lax.all_gather(panel_v, "col", axis=2, tiled=True)
    masked_panel = mask_columns(panel_u, panel_rank[:, :, None, None])
    solved = dot("pab,ptbr->tpar", inverse_block, raw_v).astype(BF16)
    owner = targets // rows_here
    local = targets - owner * rows_here
    sides = jnp.where(
        (owner == me)[:, None, None, None], jnp.take(solved, local, axis=0), jnp.zeros((), BF16)
    )
    side_v = lax.psum(sides, "row")
    part = dot("tpar,cpas->ctprs", solved, side_v).astype(BF16)
    cross = lax.psum_scatter(part, "col", scatter_dimension=0, tiled=True)[0]
    whole_u = lax.all_gather(masked_panel, "col", axis=2, tiled=True)
    target = column_tiles[0]
    mine = target // rows_here
    pick_u = lax.dynamic_index_in_dim(
        whole_u, target - mine * rows_here, 1, keepdims=False
    )
    side_u = lax.psum(jnp.where(mine == me, pick_u, jnp.zeros_like(pick_u)), "row")

    side_small = dot("pas,ak->psk", side_u, sketch).astype(BF16)
    tile_u = slab_u[:, 0]
    tile_v = slab_v[:, 0]
    tile_u = mask_columns(tile_u, slab_rank[:, 0][:, None, None])
    small_v = dot("tar,ak->trk", tile_v, sketch).astype(BF16)
    small_u = (-dot("tprs,psk->tprk", cross, side_small)).astype(BF16)
    image = dot("tar,trk->tak", tile_u, small_v)
    for p in range(panels):
        image = image + dot("tar,trk->tak", whole_u[p], small_u[:, p])
    gram = jnp.einsum(
        "tak,tal->tkl",
        image,
        image,
        precision=lax.Precision.HIGHEST,
        preferred_element_type=F32,
    )
    gram = gram + jnp.eye(gram.shape[1], dtype=F32)
    inverse = invert_factor(gram)
    basis = jnp.einsum(
        "tak,tlk->tal",
        image,
        inverse,
        precision=lax.Precision.HIGHEST,
        preferred_element_type=F32,
    )
    basis_out = (basis * jnp.sqrt(F32(width))).astype(BF16)
    basis_low = basis.astype(BF16)
    project = dot("tar,tak->trk", tile_u, basis_low).astype(BF16)
    coeff = dot("tar,trk->tak", tile_v, project)
    for p in range(panels):
        project = dot("tar,tak->trk", whole_u[p], basis_low).astype(BF16)
        inner = dot("trs,trk->tsk", cross[:, p], project).astype(BF16)
        coeff = coeff - dot("as,tsk->tak", side_u[p], inner)
    return basis_out[:, None], coeff.astype(BF16)[:, None]


def solution(mesh):
    in_specs = (
        P("row", "col", None, None),
        P("row", "col", None, None),
        P("row", "col"),
        P(None, "row", "col", None),
        P(None, "row", "col", None),
        P(None, "row"),
        P(None, "col", None),
        P("col"),
        P(),
    )
    out_specs = (P("row", "col", None, None), P("row", "col", None, None))
    return jax.shard_map(shards, mesh=mesh, in_specs=in_specs, out_specs=out_specs, check_vma=False)
```

```python
import functools

import jax
import jax.numpy as jnp
from jax import lax
from jax.experimental import pallas as pl
from jax.experimental.pallas import tpu as pltpu
from jax.sharding import PartitionSpec as P

F32 = jnp.float32
BF16 = jnp.bfloat16
GROUP = 4
BLOCK = 128


def mask_columns(factor, rank):
    columns = jnp.arange(factor.shape[-1], dtype=jnp.int32)
    keep = (columns < rank).astype(factor.dtype)
    return factor * keep


def invert_blocks(blocks):
    n = blocks[0].shape[0]
    lane_row = lax.broadcasted_iota(jnp.int32, (1, n), 1)
    many = range(len(blocks))
    left = list(blocks)
    done = [[] for _ in many]
    top = 0
    for j in range(0, n, GROUP):
        start = (j // 8) * 8
        if start > top:
            left = [t[start - top :] for t in left]
            top = start
        rows = n - top
        at = j - top
        row_index = lax.broadcasted_iota(jnp.int32, (rows, n), 0) + top
        lane = lax.broadcasted_iota(jnp.int32, (rows, n), 1)
        inside = (lane >= j) & (lane < j + GROUP)
        for b in many:
            t = left[b]
            col = [
                jnp.broadcast_to(t[:, j + s : j + s + 1], (rows, n)) for s in range(GROUP)
            ]
            row = [t[at + s : at + s + 1, :] for s in range(GROUP)]
            new = jnp.where(inside, 0.0, t)
            for s in range(GROUP):
                pivot = col[s][at + s : at + s + 1, :]
                comb = jnp.where(lane_row == j + s, 1.0, row[s])
                times = jnp.where(row_index > j + s, col[s] / pivot, 0.0)
                for u in range(s + 1, GROUP):
                    col[u] = col[u] - times * col[u][at + s : at + s + 1, :]
                    here = jnp.where(lane_row == j + s, 0.0, row[u])
                    row[u] = here - times[at + u : at + u + 1, :] * comb
                later = (lane_row > j + s) & (lane_row < j + GROUP)
                new = new - times * jnp.where(later, 0.0, comb)
                done[b].append(
                    jnp.where(lane_row <= j + s, comb, 0.0) * lax.rsqrt(pivot)
                )
            left[b] = new
    return [jnp.concatenate(rows_of, axis=0) for rows_of in done]


def full_dot(a, b, dims):
    return lax.dot_general(
        a, b, (dims, ((), ())), precision=lax.Precision.HIGHEST, preferred_element_type=F32
    )


def factor_kernel(gram_ref, out_ref):
    tiles = gram_ref.shape[0]
    n = gram_ref.shape[1]
    half = n // 2
    many = range(tiles)
    first = invert_blocks([gram_ref[b, :half, :half] for b in many])
    lower = [full_dot(gram_ref[b, half:, :half], first[b], ((1,), (1,))) for b in many]
    rest = [
        gram_ref[b, half:, half:] - full_dot(lower[b], lower[b], ((1,), (1,))) for b in many
    ]
    second = invert_blocks(rest)
    for b in many:
        corner = full_dot(lower[b], first[b], ((1,), (0,)))
        out_ref[b, :half, :half] = first[b]
        out_ref[b, :half, half:] = jnp.zeros((half, half), F32)
        out_ref[b, half:, :half] = -full_dot(second[b], corner, ((1,), (0,)))
        out_ref[b, half:, half:] = second[b]


def invert_factor(gram):
    tiles, n, _ = gram.shape
    step = 2 if tiles % 2 == 0 else 1
    return pl.pallas_call(
        factor_kernel,
        grid=(tiles // step,),
        out_shape=jax.ShapeDtypeStruct(gram.shape, F32),
        in_specs=[pl.BlockSpec((step, n, n), lambda i: (i, 0, 0))],
        out_specs=pl.BlockSpec((step, n, n), lambda i: (i, 0, 0)),
        compiler_params=pltpu.CompilerParams(vmem_limit_bytes=32 * 1024 * 1024),
        cost_estimate=pl.CostEstimate(
            flops=tiles * n * n * n, bytes_accessed=2 * gram.size * 4, transcendentals=0
        ),
    )(gram)


def exchange_kernel(
    n_row, n_col, v_ref, u_ref, inv_ref, goal_ref,
    u_all, s_all, side_u, side_v,
    v_all, acc_u, acc_v, core_u, core_v, step_u, step_v,
    v_send, v_recv, u_send, u_recv, s_send, s_recv,
    ru_send, ru_recv, rv_send, rv_recv,
):
    row = lax.axis_index("row")
    col = lax.axis_index("col")
    panels, tiles, height, rank = v_ref.shape
    half = n_col // 2
    quarter = half // 2
    bits = [1 << k for k in range(1, n_row.bit_length() - 1)]

    def across(bit):
        return row + bit * (1 - 2 * lax.rem(row // bit, 2))

    def remote(src, dst, send, recv, **where):
        return pltpu.make_async_remote_copy(
            src_ref=src, dst_ref=dst, send_sem=send, recv_sem=recv,
            device_id=where, device_id_type=pl.DeviceIdType.MESH,
        )

    barrier = pltpu.get_barrier_semaphore()
    for d in range(1, n_col):
        pl.semaphore_signal(
            barrier, inc=1, device_id={"col": lax.rem(col + d, n_col)},
            device_id_type=pl.DeviceIdType.MESH,
        )
    for bit in [1] + bits:
        pl.semaphore_signal(
            barrier, inc=1, device_id={"row": across(bit)},
            device_id_type=pl.DeviceIdType.MESH,
        )
    pl.semaphore_wait(barrier, n_col - 1 + 1 + len(bits))

    def hop(whole, send, recv, s):
        right = remote(
            whole.at[jnp.maximum(col - s, 0)], whole.at[jnp.maximum(col - s, 0)],
            send.at[0, s], recv.at[0, s], col=jnp.minimum(col + 1, n_col - 1),
        )
        left = remote(
            whole.at[jnp.minimum(col + s, n_col - 1)], whole.at[jnp.minimum(col + s, n_col - 1)],
            send.at[1, s], recv.at[1, s], col=jnp.maximum(col - 1, 0),
        )
        return right, left

    def hop_start(whole, send, recv, s):
        right, left = hop(whole, send, recv, s)

        @pl.when((col - s >= 0) & (col + 1 < n_col))
        def _():
            right.start()

        @pl.when((col + s < n_col) & (col >= 1))
        def _():
            left.start()

    def hop_recv(whole, send, recv, s):
        right, left = hop(whole, send, recv, s)

        @pl.when(col - 1 - s >= 0)
        def _():
            right.wait_recv()

        @pl.when(col + 1 + s < n_col)
        def _():
            left.wait_recv()

    def hop_end(whole, send, recv, s):
        right, left = hop(whole, send, recv, s)

        @pl.when((col - s >= 0) & (col + 1 < n_col))
        def _():
            right.wait_send()

        @pl.when((col + s < n_col) & (col >= 1))
        def _():
            left.wait_send()

    v_all[col] = v_ref[...]
    for s in range(n_col - 1):
        hop_start(v_all, v_send, v_recv, s)
        if s == 0:
            u_all[col] = u_ref[...]
        hop_recv(v_all, v_send, v_recv, s)
    for s in range(n_col - 1):
        hop_end(v_all, v_send, v_recv, s)

    hop_start(u_all, u_send, u_recv, 0)
    for p in range(panels):
        for t in range(tiles):
            raw = jnp.concatenate([v_all[z, p, t] for z in range(n_col)], axis=0)
            s_all[col, p, t] = jnp.dot(
                inv_ref[p], raw, preferred_element_type=F32
            ).astype(BF16)
    for s in range(n_col - 2):
        hop_recv(u_all, u_send, u_recv, s)
        hop_start(u_all, u_send, u_recv, s + 1)
    hop_start(s_all, s_send, s_recv, 0)
    hop_recv(u_all, u_send, u_recv, n_col - 2)
    for s in range(n_col - 1):
        hop_end(u_all, u_send, u_recv, s)

    def chosen(goal, source):
        total = None
        for t in range(tiles):
            hit = jnp.where(goal[0:1, :] == row * tiles + t, 1.0, 0.0)
            term = source[t].astype(F32) * hit
            total = term if total is None else total + term
        return total.astype(BF16)

    def pick(acc, whole):
        goal = goal_ref[...]
        for z in range(n_col):
            for p in range(panels):
                acc[z, p] = chosen(goal, [whole[z, p, t] for t in range(tiles)])

    def spread(acc, out, core_buf, step_buf, send, recv, between):
        core = lax.rem(row, 2)
        mine = core * half
        first = remote(
            acc.at[pl.ds((1 - core) * half, half)], core_buf, send.at[0], recv.at[0],
            row=across(1),
        )
        first.start()
        first.wait()
        for k in range(half):
            acc[mine + k] = acc[mine + k] + core_buf[k]
        for step, bit in enumerate(bits):
            copies = []
            for piece in range(2):
                to = bit if piece == 0 else bits[len(bits) - 1 - step]
                copies.append(
                    remote(
                        acc.at[pl.ds(mine + piece * quarter, quarter)],
                        step_buf.at[step, piece],
                        send.at[1 + 2 * step + piece],
                        recv.at[1 + 2 * step + piece],
                        row=across(to),
                    )
                )
                copies[-1].start()
            between(step)
            for piece in range(2):
                copies[piece].wait()
                for k in range(quarter):
                    at = mine + piece * quarter + k
                    acc[at] = acc[at] + step_buf[step, piece, k]
        last = remote(
            acc.at[pl.ds(mine, half)], out.at[pl.ds(mine, half)],
            send.at[1 + 2 * len(bits)], recv.at[1 + 2 * len(bits)], row=across(1),
        )
        last.start()
        for k in range(half):
            out[mine + k] = acc[mine + k]
        last.wait()

    def next_hop(step):
        if step + 1 < n_col - 1:
            hop_recv(s_all, s_send, s_recv, step)
            hop_start(s_all, s_send, s_recv, step + 1)

    pick(acc_u, u_all)
    spread(acc_u, side_u, core_u, step_u, ru_send, ru_recv, next_hop)
    for s in range(len(bits), n_col - 1):
        if s > len(bits):
            hop_start(s_all, s_send, s_recv, s)
        hop_recv(s_all, s_send, s_recv, s)
    for s in range(n_col - 1):
        hop_end(s_all, s_send, s_recv, s)
    pick(acc_v, s_all)
    spread(acc_v, side_v, core_v, step_v, rv_send, rv_recv, lambda step: None)


def exchange(n_row, n_col, panel_v, masked_panel, inverse_block, column_tiles):
    panels, tiles, height, rank = panel_v.shape
    goal = jnp.broadcast_to(column_tiles.reshape(1, 1), (8, rank)).astype(jnp.int32)
    half, quarter = n_col // 2, n_col // 4
    steps = n_row.bit_length() - 2
    side = (n_col, panels, height, rank)
    dma = pltpu.SemaphoreType.DMA
    vmem = pl.BlockSpec(memory_space=pltpu.VMEM)
    spread_buffers = [
        pltpu.VMEM((half,) + side[1:], BF16),
        pltpu.VMEM((steps, 2, quarter) + side[1:], BF16),
    ]
    return pl.pallas_call(
        lambda *refs: exchange_kernel(n_row, n_col, *refs),
        out_shape=[
            jax.ShapeDtypeStruct((n_col,) + panel_v.shape, BF16),
            jax.ShapeDtypeStruct((n_col,) + panel_v.shape, BF16),
            jax.ShapeDtypeStruct(side, BF16),
            jax.ShapeDtypeStruct(side, BF16),
        ],
        in_specs=[vmem] * 4,
        out_specs=[vmem] * 4,
        scratch_shapes=[
            pltpu.VMEM((n_col,) + panel_v.shape, BF16),
            pltpu.VMEM(side, BF16),
            pltpu.VMEM(side, BF16),
            spread_buffers[0],
            spread_buffers[0],
            spread_buffers[1],
            spread_buffers[1],
        ]
        + [dma((2, n_col - 1))] * 6
        + [dma((2 + 2 * steps,))] * 4,
        compiler_params=pltpu.CompilerParams(
            collective_id=0, has_side_effects=True, vmem_limit_bytes=60 * 1024 * 1024
        ),
    )(panel_v, masked_panel, inverse_block, goal)


def dot(spec, a, b):
    return jnp.einsum(spec, a, b, preferred_element_type=F32)


def shards(
    n_row, n_col,
    slab_u, slab_v, slab_rank, panel_u, panel_v, panel_rank, inverse_block, column_tiles, sketch
):
    tiles = panel_u.shape[1]
    panels = panel_u.shape[0]
    width, rank = sketch.shape
    masked_panel = mask_columns(panel_u, panel_rank[:, :, None, None])
    u_all, s_all, side_u, side_v = exchange(
        n_row, n_col, panel_v, masked_panel, inverse_block, column_tiles
    )
    whole_u = u_all.transpose(1, 2, 0, 3, 4).reshape(panels, tiles, width, rank)
    side_u = side_u.transpose(1, 0, 2, 3).reshape(panels, width, rank)
    whole_s = s_all.transpose(1, 2, 0, 3, 4).reshape(panels, tiles, width, rank)
    side_v = side_v.transpose(1, 0, 2, 3).reshape(panels, width, rank)
    cross = dot("ptar,pas->ptrs", whole_s, side_v).astype(BF16)
    update = dot("pas,ptrs->ptar", side_u, cross).astype(BF16)
    tile_u = slab_u[:, 0]
    tile_v = slab_v[:, 0]
    tile_u = mask_columns(tile_u, slab_rank[:, 0][:, None, None])
    small_v = dot("tar,ak->trk", tile_v, sketch).astype(BF16)
    small_u = (-dot("ptar,ak->ptrk", update, sketch)).astype(BF16)
    image = dot("tar,trk->tak", tile_u, small_v)
    for p in range(panels):
        image = image + dot("tar,trk->tak", whole_u[p], small_u[p])
    gram = jnp.einsum(
        "tak,tal->tkl",
        image,
        image,
        precision=lax.Precision.HIGHEST,
        preferred_element_type=F32,
    )
    gram = gram + jnp.eye(gram.shape[1], dtype=F32)
    inverse = invert_factor(gram)
    basis = jnp.einsum(
        "tak,tlk->tal",
        image,
        inverse,
        precision=lax.Precision.HIGHEST,
        preferred_element_type=F32,
    )
    basis_out = (basis * jnp.sqrt(F32(width))).astype(BF16)
    basis_low = basis.astype(BF16)
    project = dot("tar,tak->trk", tile_u, basis_low).astype(BF16)
    coeff = dot("tar,trk->tak", tile_v, project)
    for p in range(panels):
        project = dot("tar,tak->trk", whole_u[p], basis_low).astype(BF16)
        coeff = coeff - dot("tar,trk->tak", update[p], project)
    return basis_out[:, None], coeff.astype(BF16)[:, None]


def solution(mesh):
    in_specs = (
        P("row", "col", None, None),
        P("row", "col", None, None),
        P("row", "col"),
        P(None, "row", "col", None),
        P(None, "row", "col", None),
        P(None, "row"),
        P(None, "col", None),
        P("col"),
        P(),
    )
    out_specs = (P("row", "col", None, None), P("row", "col", None, None))
    body = functools.partial(shards, mesh.shape["row"], mesh.shape["col"])
    return jax.shard_map(body, mesh=mesh, in_specs=in_specs, out_specs=out_specs, check_vma=False)
```
